256 devices in a mesh: section: 16 (over z_lo, x), tp: 16 (over y, z_hi, core).
Axes of the slice: x: 4, y: 4, z: 8 (z_hi: 2, z_lo: 4; z = z_hi * 4 + z_lo), core: 2. Of those that a mesh axis runs over, the one named last changes fastest.
Arguments:
- fwd_in: bfloat16 [16, 128, 4096], P('section', None, 'tp'), may hold values from -6 to 6
- grad_in: bfloat16 [16, 128, 4096], P('section', None, 'tp'), may hold values from -6 to 6
- parked_rows: bfloat16 [16, 2, 128, 4096], P('section', None, None, 'tp'), may hold values from -6 to 6
- parked_query: bfloat16 [16, 2, 128, 4096], P('section', None, None, 'tp'), may hold values from -16 to 16
- parked_keyval: bfloat16 [16, 2, 128, 1024], P('section', None, None, 'tp'), may hold values from -16 to 16
- norm_gain: float32 [16, 4096], P('section'), may hold values from 0.1 to 1.9
- w_query: bfloat16 [16, 4096, 4096], P('section', None, 'tp'), may hold values from -0.09375 to 0.09375
- w_keyval: bfloat16 [16, 4096, 1024], P('section', None, 'tp'), may hold values from -0.09375 to 0.09375
- w_out: bfloat16 [16, 4096, 4096], P('section', 'tp'), may hold values from -0.09375 to 0.09375
Outputs:
- fwd_out: bfloat16 [16, 128, 4096], P('section', None, 'tp')
- grad_out: bfloat16 [16, 128, 4096], P('section', None, 'tp')
- evicted_rows: bfloat16 [16, 2, 128, 4096], P('section', None, None, 'tp')
- evicted_query: bfloat16 [16, 2, 128, 4096], P('section', None, None, 'tp')
- evicted_keyval: bfloat16 [16, 2, 128, 1024], P('section', None, None, 'tp')
The draws below stay inside these ranges and needn't reach their ends.
All inputs are finite; a program needn't handle non-finite values.
Results may differ from the reference program's by a relative error of at most 0.03.
Values may be sent and summed in bfloat16 or wider, within the bound.
No kernel may reach another device: no remote copies, remote signals or barrier semaphores. Data moves between devices by JAX's collectives and lax.ppermute only.
A program may use at most 64 MiB of HBM per device.

```python
import jax
import jax.numpy as jnp
from jax import lax

D = 4096
HQ = 32
HK = 4
HD = 128
SEQ = 128
TICKS = 2
N_SECTION = 16


def draw_parked_keyval(key, part):
    key = jax.random.fold_in(key, 7)
    draws = jax.random.normal(key, (N_SECTION, TICKS, SEQ, 2 * HK * HD), jnp.float32)
    return jnp.clip(draws, -16.0, 16.0).astype(jnp.bfloat16)


def draw_parked_query(key, part):
    key = jax.random.fold_in(key, 9)
    draws = jax.random.normal(key, (N_SECTION, TICKS, SEQ, HQ * HD), jnp.float32)
    return jnp.clip(draws, -16.0, 16.0).astype(jnp.bfloat16)


def level_of(key, extent, cuts, least, top_value):
    def one(axis_at, blocks):
        steps = jax.random.uniform(jax.random.fold_in(jax.random.fold_in(key, 6), axis_at), (blocks,), jnp.float32, least / len(cuts), top_value / len(cuts))
        return jnp.repeat(jnp.exp(steps), extent[axis_at] // blocks).reshape((-1,) + (1,) * (len(extent) - axis_at - 1))

    level = one(*cuts[0])
    for cut in cuts[1:]:
        level = level * one(*cut)
    return level


def noise(own_key, shape, spread, reach, split=(), kind=jnp.bfloat16):
    loudness = level_of(own_key, shape, split, -0.22, 0.18) if split else 1.0
    entries = jax.random.normal(own_key, shape, jnp.float32) * spread * loudness
    return jnp.minimum(jnp.maximum(entries, -reach), reach).astype(kind)


def setup_inputs(seed: int = 0) -> dict:
    key_list = jax.random.split(jax.random.key(seed), 10)
    return {
        "fwd_in": noise(key_list[0], (N_SECTION, SEQ, D), 1.0, 6.0, ((0, 16), (2, 16))),
        "grad_in": noise(key_list[1], (N_SECTION, SEQ, D), 1.0, 6.0, ((0, 16), (2, 16))),
        "parked_rows": noise(key_list[2], (N_SECTION, TICKS, SEQ, D), 1.0, 6.0, ((0, 16), (3, 16))),
        "parked_query": draw_parked_query(jax.random.fold_in(key_list[9], 71), 0),
        "parked_keyval": draw_parked_keyval(jax.random.fold_in(key_list[9], 71), 0),
        "norm_gain": jnp.clip(1.0 + 0.18 * jax.random.normal(key_list[5], (N_SECTION, D), jnp.float32), 0.1, 1.9),
        "w_query": noise(key_list[6], (N_SECTION, D, HQ * HD), D ** -0.5, 0.09375, ((0, 16), (2, 16))),
        "w_keyval": noise(key_list[7], (N_SECTION, D, 2 * HK * HD), D ** -0.5, 0.09375, ((0, 16), (2, 16))),
        "w_out": noise(key_list[8], (N_SECTION, HQ * HD, D), (HQ * HD) ** -0.5, 0.09375, ((0, 16), (1, 16))),
    }


epsilon = 1e-05

def normalize(block_rows):
    values_f = block_rows.astype(jnp.float32)
    inverse = lax.rsqrt(lax.optimization_barrier(jnp.mean(values_f * values_f, axis=-1, keepdims=True)) + epsilon)
    return (values_f * inverse, inverse)

def causal_softmax(query_heads, key_heads):
    scores = jnp.einsum('shd,thd->hst', query_heads.astype(jnp.float32), key_heads.astype(jnp.float32)) * HD ** (-0.5)
    length = query_heads.shape[0]
    position = jnp.arange(length)
    causal = position[:, None] >= position[None, :]
    scores = jnp.where(causal[None], scores, -1e+30)
    highest = lax.optimization_barrier(jnp.max(scores, axis=-1, keepdims=True))
    weights = jnp.exp(scores - highest)
    return weights / lax.optimization_barrier(jnp.sum(weights, axis=-1, keepdims=True))

def split_heads(keyval):
    length = keyval.shape[0]
    repeat_count = HQ // HK
    key_heads = keyval[:, :HK * HD].reshape(length, HK, HD)
    value_heads = keyval[:, HK * HD:].reshape(length, HK, HD)
    return (jnp.repeat(key_heads, repeat_count, axis=1), jnp.repeat(value_heads, repeat_count, axis=1))

def layer_forward(inputs, gain, w_query, w_keyval, w_out):
    length = inputs.shape[0]
    normed_f, inverse = normalize(inputs)
    normed = (normed_f * gain.astype(jnp.float32)).astype(jnp.bfloat16)
    query = jnp.dot(normed, w_query, preferred_element_type=jnp.float32).astype(jnp.bfloat16)
    keyval = jnp.dot(normed, w_keyval, preferred_element_type=jnp.float32).astype(jnp.bfloat16)
    key_rep, value_rep = split_heads(keyval)
    probs = causal_softmax(query.reshape(length, HQ, HD), key_rep)
    probs_low = probs.astype(jnp.bfloat16).astype(jnp.float32)
    mixed = jnp.einsum('hst,thd->shd', probs_low, value_rep.astype(jnp.float32)).astype(jnp.bfloat16)
    mixed = mixed.reshape(length, HQ * HD)
    output = inputs.astype(jnp.float32) + jnp.dot(mixed, w_out, preferred_element_type=jnp.float32)
    return (output.astype(jnp.bfloat16), query, keyval)

def layer_backward(inputs, gain, query, keyval, w_query, w_keyval, w_out, cotangent):
    length = inputs.shape[0]
    head_grads = jnp.dot(cotangent, w_out.T, preferred_element_type=jnp.float32).astype(jnp.bfloat16)
    key_rep, value_rep = split_heads(keyval)
    query_heads = query.reshape(length, HQ, HD).astype(jnp.float32)
    probs = causal_softmax(query_heads, key_rep)
    grad_heads = head_grads.reshape(length, HQ, HD).astype(jnp.float32)
    grad_prob = jnp.einsum('shd,thd->hst', grad_heads, value_rep.astype(jnp.float32))
    delta_rows = lax.optimization_barrier(jnp.sum(grad_prob * probs, axis=-1, keepdims=True))
    dscore = (probs * (grad_prob - delta_rows) * HD ** (-0.5)).astype(jnp.bfloat16).astype(jnp.float32)
    dquery = jnp.einsum('hst,thd->shd', dscore, key_rep.astype(jnp.float32)).astype(jnp.bfloat16)
    dquery = dquery.reshape(length, HQ * HD)
    dkey_heads = jnp.einsum('hst,shd->thd', dscore, query_heads)
    probs_low = probs.astype(jnp.bfloat16).astype(jnp.float32)
    dvalue_heads = jnp.einsum('hst,shd->thd', probs_low, grad_heads)
    repeat_count = HQ // HK
    dkey = dkey_heads.reshape(length, HK, repeat_count, HD).sum(axis=2).reshape(length, HK * HD)
    dvalue = dvalue_heads.reshape(length, HK, repeat_count, HD).sum(axis=2).reshape(length, HK * HD)
    dkeyval = jnp.concatenate([dkey, dvalue], axis=1).astype(jnp.bfloat16)
    dnormed = jnp.dot(dquery, w_query.T, preferred_element_type=jnp.float32)
    dnormed = dnormed + jnp.dot(dkeyval, w_keyval.T, preferred_element_type=jnp.float32)
    normed_f, inverse = normalize(inputs)
    scaled = dnormed * gain.astype(jnp.float32)
    result = cotangent.astype(jnp.float32) + inverse * (scaled - normed_f * lax.optimization_barrier(jnp.mean(scaled * normed_f, axis=-1, keepdims=True)))
    return result.astype(jnp.bfloat16)

def reference(fwd_in, grad_in, parked_rows, parked_query, parked_keyval, norm_gain, w_query, w_keyval, w_out):
    section_count = N_SECTION
    inputs_now = [fwd_in[index] for index in range(section_count)]
    grads_now = [grad_in[index] for index in range(section_count)]
    produced = [[] for index in range(section_count)]
    outs_forward = []
    outs_backward = []
    for tick_index in range(TICKS):
        outs_forward = []
        outs_backward = []
        for section_index in range(section_count):
            mirror = section_count - 1 - section_index
            layer_out, query, keyval = layer_forward(inputs_now[section_index], norm_gain[section_index], w_query[section_index], w_keyval[section_index], w_out[section_index])
            produced[section_index].append((inputs_now[section_index], query, keyval))
            input_grad = layer_backward(parked_rows[mirror, tick_index], norm_gain[section_index], parked_query[mirror, tick_index], parked_keyval[mirror, tick_index], w_query[section_index], w_keyval[section_index], w_out[section_index], grads_now[section_index])
            outs_forward.append(layer_out)
            outs_backward.append(input_grad)
        if tick_index + 1 < TICKS:
            zero_block = jnp.zeros_like(fwd_in[0])
            inputs_now = [zero_block] + outs_forward[:-1]
            grads_now = outs_backward[1:] + [zero_block]
    evicted = []
    for member in range(3):
        evicted.append(jnp.stack([jnp.stack([produced[section_count - 1 - index][tick_index][member] for tick_index in range(TICKS)]) for index in range(section_count)]))
    return (jnp.stack(outs_forward), jnp.stack(outs_backward), evicted[0], evicted[1], evicted[2])
```

```python
import jax
import jax.numpy as jnp
from jax import lax
from jax.sharding import PartitionSpec as P

HD = 128
TICKS = 2
EPS = 1e-05
BF = jnp.bfloat16
F32 = jnp.float32
HB = 256
SEQ = 128


def tp_perm(x, f):
    return lax.ppermute(x, "tp", [(t, f(t)) for t in range(16)])


def both_perm(x, fs, ft):
    return lax.ppermute(
        x, ("section", "tp"), [(s * 16 + t, fs(s) * 16 + ft(t)) for s in range(16) for t in range(16)]
    )


def mirror(s):
    return 15 - s


def swap_core(x):
    return tp_perm(x, lambda t: t ^ 1)


def swap_z(x):
    return tp_perm(x, lambda t: t ^ 2)


def swap_y(x, j):
    return tp_perm(x, lambda t: t ^ (4 * j))


def to_group(t):
    y, z, c = t // 4, t // 2 % 2, t % 2
    return (2 * (y % 2) + z) * 4 + c * 2 + y // 2


def from_group(t):
    y, z, c = t // 4, t // 2 % 2, t % 2
    return (2 * c + y // 2) * 4 + (y % 2) * 2 + z


def gather_yc(x512):
    half = jnp.concatenate([x512] + [swap_y(x512, j) for j in (1, 2, 3)], axis=1)
    return jnp.concatenate([half, swap_core(half)], axis=1)


def hi_lo(s):
    hi = s.astype(BF)
    return jnp.concatenate([hi, (s - hi.astype(F32)).astype(BF)], axis=1)


def scatter_cy(term, s=None):
    keep, send = term[:, :2048], term[:, 2048:].astype(BF)
    if s is None:
        h = keep + swap_core(send).astype(F32)
        acc = h[:, :512]
        for j in (1, 2, 3):
            acc = acc + swap_y(h[:, 512 * j : 512 * j + 512].astype(BF), j).astype(F32)
        return acc
    got = swap_core(jnp.concatenate([send, hi_lo(s)], axis=1)).astype(F32)
    h = keep + got[:, :2048]
    s = s + got[:, 2048:2049] + got[:, 2049:2050]
    acc, tot = h[:, :512], s
    for j in (1, 2, 3):
        got = swap_y(
            jnp.concatenate([h[:, 512 * j : 512 * j + 512].astype(BF), hi_lo(s)], axis=1), j
        ).astype(F32)
        acc = acc + got[:, :512]
        tot = tot + got[:, 512:513] + got[:, 513:514]
    return acc, tot


def flip(x):
    return jnp.concatenate([x[:, HB:], x[:, :HB]], axis=1)


def softmax_causal(q, k):
    scores = lax.dot_general(q, k, (((1,), (1,)), ((), ())), preferred_element_type=F32) * HD**-0.5
    row = lax.broadcasted_iota(jnp.int32, scores.shape, 0)
    col = lax.broadcasted_iota(jnp.int32, scores.shape, 1)
    scores = jnp.where(row >= col, scores, -1e30)
    w = jnp.exp(scores - jnp.max(scores, axis=-1, keepdims=True))
    return w / jnp.sum(w, axis=-1, keepdims=True)


def nt(a, b):
    return lax.dot_general(a, b, (((1,), (1,)), ((), ())), preferred_element_type=F32)


def tn(a, b):
    return lax.dot_general(a, b, (((0,), (0,)), ((), ())), preferred_element_type=F32)


def nn(a, b):
    return jnp.dot(a, b, preferred_element_type=F32)


def inverse_rms(x):
    f = x.astype(F32)
    return lax.rsqrt(jnp.mean(f * f, axis=-1, keepdims=True) + EPS)


def local(
    fwd_in, grad_in, parked_rows, parked_query, parked_keyval, norm_gain, w_query, w_keyval, w_out
):
    t = lax.axis_index("tp")
    core = t % 2
    ks = jnp.array(
        [ky * 4 + kz * 2 + kc for kc in range(2) for ky in range(4) for kz in range(2)], jnp.int32
    )
    order = jnp.bitwise_xor(ks, t)
    gain = norm_gain[0].reshape(4096, 1)
    wq = (w_query[0].astype(F32) * gain).astype(BF)
    wkv = (w_keyval[0].astype(F32) * gain).astype(BF)
    wqkv = jnp.concatenate([wq, wkv], axis=1)
    wqkv = jnp.take(wqkv.reshape(16, HB, 320), order, axis=0).reshape(4096, 320)
    wo = jnp.take(w_out[0].reshape(HB, 16, HB), order, axis=1).reshape(HB, 4096)

    def by_core(a, b):
        return jnp.where(core == 0, a, b)

    def kv_exchange(kv, move):
        other = swap_core(kv)
        pair = by_core(
            jnp.concatenate([kv, other], axis=-1), jnp.concatenate([other, kv], axis=-1)
        )
        mine = move(pair)
        other = swap_core(mine)
        return by_core(mine, other), by_core(other, mine)

    def dkv_exchange(dk, dv):
        part = by_core(dk, dv) + swap_core(by_core(dv, dk).astype(BF)).astype(F32)
        part = tp_perm(part.astype(BF), from_group)
        other = swap_core(by_core(part[:, 64:], part[:, :64])).astype(F32)
        return (by_core(part[:, :64], part[:, 64:]).astype(F32) + other).astype(BF)

    x = fwd_in[0]
    g = grad_in[0]
    x512 = jnp.concatenate([x, swap_z(x)], axis=1)
    g512 = jnp.concatenate([g, swap_z(g)], axis=1)
    stash_q = both_perm(parked_query[0], mirror, lambda i: i)
    stash_k, stash_v = kv_exchange(parked_keyval[0], lambda v: both_perm(v, mirror, to_group))
    evicted = []
    for tick in range(TICKS):
        last = tick == TICKS - 1
        u = parked_rows[0, tick]
        u512 = jnp.concatenate(
            [both_perm(u, mirror, lambda i: i), both_perm(u, mirror, lambda i: i ^ 2)], axis=1
        )
        xf = gather_yc(x512)
        inv = inverse_rms(xf)
        qkv = (nn(xf, wqkv) * inv).astype(BF)
        q, kv = qkv[:, :HB], qkv[:, HB:]
        key, val = kv_exchange(kv, lambda v: tp_perm(v, to_group))
        mixed = []
        for h in range(2):
            p = softmax_causal(q[:, h * HD : h * HD + HD], key)
            mixed.append(nn(p.astype(BF), val))
        mixed = jnp.concatenate(mixed, axis=1).astype(BF)
        facc = scatter_cy(nn(mixed, wo))
        gf = gather_yc(g512)
        hg = nt(gf, wo).astype(BF)
        dk = dv = 0.0
        dqs = []
        sk, sv = stash_k[tick], stash_v[tick]
        for h in range(2):
            sq = stash_q[tick][:, h * HD : h * HD + HD]
            hgh = hg[:, h * HD : h * HD + HD]
            p = softmax_causal(sq, sk)
            dp = nt(hgh, sv)
            delta = jnp.sum(dp * p, axis=-1, keepdims=True)
            ds = (p * (dp - delta) * HD**-0.5).astype(BF)
            dqs.append(nn(ds, sk))
            dk = dk + tn(ds, sq)
            dv = dv + tn(p.astype(BF), hgh)
        dq = jnp.concatenate(dqs, axis=1).astype(BF)
        dkv = dkv_exchange(dk, dv)
        dn = nt(jnp.concatenate([dq, dkv], axis=1), wqkv)
        uf = gather_yc(u512)
        uinv = inverse_rms(uf)
        s = jnp.sum(dn * uf.astype(F32), axis=-1, keepdims=True) * uinv
        bacc, s = scatter_cy(dn, s)
        if not last:
            fa = facc.astype(BF)
            ft = fa.astype(F32) + flip(swap_z(fa)).astype(F32)
            a512 = (x512.astype(F32) + ft).astype(BF)
            ba = jnp.concatenate([bacc.astype(BF), hi_lo(s)], axis=1)
            got = swap_z(ba).astype(F32)
            dn512 = ba[:, :512].astype(F32) + flip(got[:, :512])
            s = s + got[:, 512:513] + got[:, 513:514]
            nhat = u512.astype(F32) * uinv
            b512 = (g512.astype(F32) + uinv * (dn512 - nhat * (s * (1.0 / 4096)))).astype(BF)
            evicted.append(both_perm(jnp.concatenate([x512[:, :HB], q, kv], axis=1), mirror, lambda i: i))
            x512 = lax.ppermute(a512, "section", [(i, i + 1) for i in range(15)])
            g512 = lax.ppermute(b512, "section", [(i + 1, i) for i in range(15)])
        else:
            ft = facc[:, :HB] + swap_z(facc[:, HB:].astype(BF)).astype(F32)
            fwd_out = (x512[:, :HB].astype(F32) + ft).astype(BF)
            got = swap_z(jnp.concatenate([bacc[:, HB:].astype(BF), hi_lo(s)], axis=1)).astype(F32)
            dn256 = bacc[:, :HB] + got[:, :HB]
            s = s + got[:, HB : HB + 1] + got[:, HB + 1 : HB + 2]
            nhat = u512[:, :HB].astype(F32) * uinv
            grad_out = (
                g512[:, :HB].astype(F32) + uinv * (dn256 - nhat * (s * (1.0 / 4096)))
            ).astype(BF)
            evicted.append(both_perm(jnp.concatenate([x512[:, :HB], q, kv], axis=1), mirror, lambda i: i))
    ev = jnp.stack(evicted)
    return (
        fwd_out[None],
        grad_out[None],
        ev[None, :, :, :HB],
        ev[None, :, :, HB : 2 * HB],
        ev[None, :, :, 2 * HB :],
    )


def solution(mesh):
    placed = (
        P("section", None, "tp"),
        P("section", None, "tp"),
        P("section", None, None, "tp"),
        P("section", None, None, "tp"),
        P("section", None, None, "tp"),
        P("section", None),
        P("section", None, "tp"),
        P("section", None, "tp"),
        P("section", "tp", None),
    )
    return jax.shard_map(
        local,
        mesh=mesh,
        in_specs=placed,
        out_specs=(
            P("section", None, "tp"),
            P("section", None, "tp"),
            P("section", None, None, "tp"),
            P("section", None, None, "tp"),
            P("section", None, None, "tp"),
        ),
        check_vma=False,
    )
```

```python
import jax
import jax.numpy as jnp
from jax import lax
from jax.experimental import pallas as pl
from jax.experimental.pallas import tpu as pltpu
from jax.sharding import PartitionSpec as P

HD = 128
EPS = 1e-05
BF = jnp.bfloat16
F32 = jnp.float32
HB = 256
SEQ = 128
D = 4096


def tp_perm(x, f):
    return lax.ppermute(x, "tp", [(t, f(t)) for t in range(16)])


def mirror_perm(x, f=lambda t: t):
    pairs = [(s * 16 + t, (15 - s) * 16 + f(t)) for s in range(16) for t in range(16)]
    return lax.ppermute(x, ("section", "tp"), pairs)


def swap_core(x):
    return tp_perm(x, lambda t: t ^ 1)


def swap_z(x):
    return tp_perm(x, lambda t: t ^ 2)


def swap_y(x, j):
    return tp_perm(x, lambda t: t ^ (4 * j))


def near_perm(x, step, f=lambda t: t):
    pairs = [(s * 16 + t, (s + step) % 16 * 16 + f(t)) for s in range(16) for t in range(16)]
    return lax.ppermute(x, ("section", "tp"), pairs)


def to_group(t, cross=0):
    y, z, c = t // 4, t // 2 % 2, t % 2
    return (2 * (y % 2) + z) * 4 + (c ^ cross) * 2 + y // 2


def from_group(t):
    y, z, c = t // 4, t // 2 % 2, t % 2
    return (2 * c + y // 2) * 4 + (y % 2) * 2 + z


def nt(a, b):
    return lax.dot_general(a, b, (((1,), (1,)), ((), ())), preferred_element_type=F32)


def tn(a, b):
    return lax.dot_general(a, b, (((0,), (0,)), ((), ())), preferred_element_type=F32)


def nn(a, b):
    return jnp.dot(a, b, preferred_element_type=F32)


def whole(shape):
    return pl.BlockSpec(shape, lambda _: (0,) * len(shape))


def part(shape, *index):
    return pl.BlockSpec(shape, lambda _: index)


SMEM = pl.BlockSpec(memory_space=pltpu.SMEM)


def call(body, ins, specs, outs, flops=0, bytes_accessed=2 << 20):
    return pl.pallas_call(
        body,
        grid=(1,),
        in_specs=specs,
        out_specs=[whole(s) for s, _ in outs],
        out_shape=[jax.ShapeDtypeStruct(s, d) for s, d in outs],
        cost_estimate=pl.CostEstimate(
            flops=flops, bytes_accessed=bytes_accessed, transcendentals=0
        ),
        compiler_params=pltpu.CompilerParams(vmem_limit_bytes=20 << 20),
    )(*ins)


def prep_body(place, wq, wkv, wo, gain, wqkv_out, wo_out, land, land_kv, q_sems, kv_sems, o_sems):
    def q_copy(k):
        rows = pl.ds(pl.multiple_of(place[k] * HB, HB), HB)
        return pltpu.make_async_copy(wq.at[rows, :], land.at[k], q_sems.at[k])

    def kv_copy(k):
        columns = pl.ds(pl.multiple_of(place[k] * HB, HB), HB)
        return pltpu.make_async_copy(wkv.at[:, columns], land_kv.at[k], kv_sems.at[k])

    def o_copy(k):
        columns = pl.ds(pl.multiple_of(place[k] * HB, HB), HB)
        return pltpu.make_async_copy(
            wo.at[:, columns], wo_out.at[:, HB * k : HB * k + HB], o_sems.at[k]
        )

    for k in range(16):
        q_copy(k).start()
        kv_copy(k).start()
    for k in range(16):
        o_copy(k).start()
    for k in range(16):
        here = jnp.broadcast_to(gain[:, pl.ds(pl.multiple_of(place[k] * HB, HB), HB)], (128, HB))
        column = jnp.transpose(here)
        wide = jnp.concatenate([column, column], axis=1)
        rows = slice(HB * k, HB * k + HB)
        q_copy(k).wait()
        wqkv_out[rows, :HB] = (land[k].astype(F32) * wide).astype(BF)
        kv_copy(k).wait()
        tall = land_kv[k].astype(F32)
        tall = jnp.concatenate([tall, tall], axis=0)
        wqkv_out[rows, HB:] = jnp.transpose(tall * here).astype(BF)
    for k in range(16):
        o_copy(k).wait()


def prepare(place, wq, wkv, wo, gain):
    hbm = pl.BlockSpec(memory_space=pltpu.HBM)
    return pl.pallas_call(
        prep_body,
        grid=(1,),
        in_specs=[SMEM, hbm, hbm, hbm, whole((1, D))],
        out_specs=[whole((D, 384)), whole((HB, D))],
        out_shape=[jax.ShapeDtypeStruct((D, 384), BF), jax.ShapeDtypeStruct((HB, D), BF)],
        scratch_shapes=[
            pltpu.VMEM((16, HB, HB), BF),
            pltpu.VMEM((16, 64, HB), BF),
            pltpu.SemaphoreType.DMA((16,)),
            pltpu.SemaphoreType.DMA((16,)),
            pltpu.SemaphoreType.DMA((16,)),
        ],
        cost_estimate=pl.CostEstimate(flops=1 << 20, bytes_accessed=20 << 20, transcendentals=0),
        compiler_params=pltpu.CompilerParams(vmem_limit_bytes=20 << 20),
    )(place, wq, wkv, wo, gain)


def pick(flag, a, b):
    return jnp.where(flag == 0, a, b)


def softmax_causal(scores):
    scores = scores * HD**-0.5
    row = lax.broadcasted_iota(jnp.int32, scores.shape, 0)
    col = lax.broadcasted_iota(jnp.int32, scores.shape, 1)
    scores = jnp.where(row >= col, scores, -1e30)
    w = jnp.exp(scores - jnp.max(scores, axis=-1, keepdims=True))
    return w / jnp.sum(w, axis=-1, keepdims=True)


def qkv_body(*refs):
    xs, w, q_out, kv_out, ev_out = refs[:8], refs[8], refs[9], refs[10], refs[11]
    acc = jnp.zeros((SEQ, 384), F32)
    squares = jnp.zeros((SEQ, 512), F32)
    for i, x in enumerate(xs):
        xv = x[...]
        xf = xv.astype(F32)
        squares = squares + xf * xf
        acc = acc + nn(xv, w[512 * i : 512 * i + 512, :])
    inv = lax.rsqrt(jnp.sum(squares, axis=-1, keepdims=True) * (1.0 / D) + EPS)
    out = acc * inv
    q_out[...] = out[:, :HB].astype(BF)
    kv_out[...] = out[:, HB : HB + 64].astype(BF)
    ev_out[:SEQ, :] = out[:, :HD].astype(BF)
    ev_out[SEQ : 2 * SEQ, :] = out[:, HD:HB].astype(BF)
    ev_out[2 * SEQ : 3 * SEQ, :] = xs[0][:, :HD]
    ev_out[3 * SEQ : 4 * SEQ, :] = xs[0][:, HD : 2 * HD]
    ev_out[4 * SEQ :, :] = jnp.transpose(out[:, HB:])[:64, :].astype(BF)


def back_body(place, *refs):
    gs, wo, sq, m1, m2, o1, o2 = refs[:8], *refs[8:14]
    dq_out, mine_out, send_out = refs[14:]
    core, z = place[16], place[17]
    acc = jnp.zeros((SEQ, HB), F32)
    for i, g in enumerate(gs):
        acc = acc + nt(g[...], wo[:, 512 * i : 512 * i + 512])
    hg = acc.astype(BF)

    def joined(a, b):
        return jnp.concatenate([pick(z, a[0], b[0]), pick(z, b[0], a[0])], axis=0)

    mine, other = joined(m1, m2), joined(o1, o2)
    key_t, val_t = pick(core, mine, other), pick(core, other, mine)
    dk = jnp.zeros((SEQ, HD), F32)
    dv = jnp.zeros((SEQ, HD), F32)
    for h in range(2):
        cut = slice(h * HD, h * HD + HD)
        q = sq[0][:, cut]
        hgh = hg[:, cut]
        p = softmax_causal(nn(q, key_t))
        dp = nn(hgh, val_t)
        delta = jnp.sum(dp * p, axis=-1, keepdims=True)
        ds = (p * (dp - delta) * HD**-0.5).astype(BF)
        dq_out[:, cut] = nt(ds, key_t).astype(BF)
        dk = dk + tn(ds, q)
        dv = dv + tn(p.astype(BF), hgh)
    mine_out[...] = pick(core, dk, dv)
    send_out[...] = pick(core, dv, dk).astype(BF)


def attend_body(place, q, kv_mine, kv_other, wo, keep_out, send_out):
    core = place[16]
    mine, other = kv_mine[...], kv_other[...]
    key, val = pick(core, mine, other), pick(core, other, mine)
    heads = []
    for h in range(2):
        p = softmax_causal(nt(q[:, h * HD : h * HD + HD], key))
        heads.append(nn(p.astype(BF), val))
    mixed = jnp.concatenate(heads, axis=1).astype(BF)
    for i in range(4):
        cut = slice(512 * i, 512 * i + 512)
        send_out[:, cut] = nn(mixed, wo[:, 2048 + 512 * i : 2560 + 512 * i]).astype(BF)
        keep_out[:, cut] = nn(mixed, wo[:, cut]).astype(BF)


def dnormed_body(place, dq, part_mine, part_other, w, *refs):
    us, keep_out, send_out, s_out, inv_out = refs[:8], refs[8], refs[9], refs[10], refs[11]
    both = part_mine[...].astype(F32) + part_other[...].astype(F32)
    lane = lax.broadcasted_iota(jnp.int32, both.shape, 1)
    dkv = jnp.where(lane // 64 == place[16], both, 0.0).astype(BF)
    d = jnp.concatenate([dq[...], dkv], axis=1)
    dots = jnp.zeros((SEQ, 512), F32)
    squares = jnp.zeros((SEQ, 512), F32)
    for i in range(8):
        dn = nt(d, w[512 * i : 512 * i + 512, :])
        u = us[i][...].astype(F32)
        dots = dots + dn * u
        squares = squares + u * u
        if i < 4:
            keep_out[:, 512 * i : 512 * i + 512] = dn.astype(BF)
        else:
            send_out[:, 512 * i - 2048 : 512 * i - 1536] = dn.astype(BF)
    inv = lax.rsqrt(jnp.sum(squares, axis=-1, keepdims=True) * (1.0 / D) + EPS)
    s = jnp.sum(dots, axis=-1, keepdims=True) * inv
    send_out[:, 2048:] = spread(s)
    s_out[...] = jnp.broadcast_to(s, (SEQ, 128))
    inv_out[...] = jnp.broadcast_to(inv, (SEQ, 128))


def spread(s):
    hi = s.astype(BF).astype(F32)
    lane = lax.broadcasted_iota(jnp.int32, (SEQ, 128), 1)
    return jnp.where(lane == 0, hi, jnp.where(lane == 1, s - hi, 0.0)).astype(BF)


def total(block):
    b = block.astype(F32)
    return b[:, 0:1] + b[:, 1:2]


def sum_core_body(f_keep, f_got, b_keep, b_got, s_in, acc_out, s_out, *sends):
    s = s_in[...][:, 0:1] + total(b_got[:, 2048:])
    wide = jnp.broadcast_to(s, (SEQ, 128))
    s_out[...] = wide
    flat = jnp.transpose(wide)[:16, :]
    hi = flat.astype(BF).astype(F32)
    row = lax.broadcasted_iota(jnp.int32, (16, 128), 0)
    flat = jnp.where(row < 8, hi, flat - hi).astype(BF)
    for j in range(4):
        cut = slice(512 * j, 512 * j + 512)
        f = f_keep[:, cut].astype(F32) + f_got[:, cut].astype(F32)
        b = b_keep[:, cut].astype(F32) + b_got[:, cut].astype(F32)
        if j == 0:
            acc_out[:, :512] = f
            acc_out[:, 512:] = b
        else:
            for i in range(4):
                sub = slice(128 * i, 128 * i + 128)
                sends[j - 1][128 * i : 128 * i + 128, :] = f[:, sub].astype(BF)
                sends[j - 1][512 + 128 * i : 640 + 128 * i, :] = b[:, sub].astype(BF)
            sends[j - 1][1024:, :] = flat


def sum_y(acc, s_in, gots, xg, u, inv_in):
    tot = []
    for i in range(8):
        sub = slice(128 * i, 128 * i + 128)
        v = acc[:, sub]
        for got in gots:
            v = v + got[sub, :].astype(F32)
        tot.append(v)
    flat = jnp.zeros((1, 128), F32)
    for got in gots:
        low = got[1024:, :].astype(F32)
        flat = flat + low[0:1, :] + low[8:9, :]
    s = s_in[...] + jnp.transpose(jnp.broadcast_to(flat, (128, 128)))
    inv = inv_in[...]
    mean = s * inv * (1.0 / D)
    for i in range(4):
        sub = slice(128 * i, 128 * i + 128)
        back = inv * (tot[4 + i] - u[:, sub].astype(F32) * mean)
        if i < 2:
            tot[i] = tot[i] + xg[:, sub].astype(F32)
            back = back + xg[:, 512 + 128 * i : 640 + 128 * i].astype(F32)
        tot[4 + i] = back
    return tot


def sum_y_mid_body(acc, s_in, g1, g2, g3, xg, u, inv_in, a_out, b_out):
    tot = sum_y(acc, s_in, (g1, g2, g3), xg, u, inv_in)
    for i in range(4):
        a_out[:, 128 * i : 128 * i + 128] = tot[i].astype(BF)
        b_out[:, 128 * i : 128 * i + 128] = tot[4 + i].astype(BF)


def sum_y_last_body(acc, s_in, g1, g2, g3, xg, u, inv_in, keep_out, send_out):
    tot = sum_y(acc, s_in, (g1, g2, g3), xg, u, inv_in)
    for i in range(2):
        sub = slice(128 * i, 128 * i + 128)
        far = slice(HB + 128 * i, HB + 128 * i + 128)
        keep_out[:, sub] = tot[i]
        keep_out[:, far] = tot[4 + i]
        send_out[:, sub] = tot[2 + i].astype(BF)
        send_out[:, far] = tot[6 + i].astype(BF)


def join_body(place, a, a_cross, b, b_cross, out):
    for at, same, cross, edge in ((0, a, a_cross, 0), (512, b, b_cross, 15)):
        for lo, hi in ((0, HB), (HB, 0)):
            v = same[:, lo : lo + HB].astype(F32) + cross[:, hi : hi + HB].astype(F32)
            v = jnp.where(place[18] == edge, 0.0, v)
            out[:, at + lo : at + lo + HB] = v.astype(BF)


def finish_body(keep, got, ev0, ev1, f_out, g_out, rows_out, query_out, keyval_out):
    f_out[...] = (keep[:, :HB] + got[:, :HB].astype(F32)).astype(BF)
    g_out[...] = (keep[:, HB:] + got[:, HB:].astype(F32)).astype(BF)
    for i, ev in enumerate((ev0, ev1)):
        query_out[i, :, :HD] = ev[:SEQ, :]
        query_out[i, :, HD:] = ev[SEQ : 2 * SEQ, :]
        rows_out[i, :, :HD] = ev[2 * SEQ : 3 * SEQ, :]
        rows_out[i, :, HD:] = ev[3 * SEQ : 4 * SEQ, :]
        keyval_out[i, :, :] = ev[4 * SEQ :, :]


def gather_y(piece):
    return [piece] + [swap_y(piece, j) for j in (1, 2, 3)]


def tie(*values):
    return list(lax.optimization_barrier(values))


def local(
    fwd_in, grad_in, parked_rows, parked_query, parked_keyval, norm_gain, w_query, w_keyval, w_out
):
    t = lax.axis_index("tp").astype(jnp.int32)
    ks = jnp.array(
        [ky * 4 + kz * 2 + kc for kc in range(2) for ky in range(4) for kz in range(2)], jnp.int32
    )
    section = lax.axis_index("section").astype(jnp.int32)
    place = jnp.concatenate([jnp.bitwise_xor(ks, t), jnp.stack([t % 2, t // 2 % 2, section])])
    core = t % 2

    def kv_pairs(kv):
        other = swap_core(kv)
        return pick(
            core,
            jnp.concatenate([kv, other], axis=-1),
            jnp.concatenate([other, kv], axis=-1),
        )

    def token(v):
        return v[:8, :128]

    x, g = fwd_in[0], grad_in[0]
    xg_z = swap_z(jnp.concatenate([x, g], axis=1))
    piece = jnp.concatenate([x, xg_z[:, :HB], g, xg_z[:, HB:]], axis=1)
    near = gather_y(piece)
    gain, _ = tie(norm_gain, token(piece))
    wqkv, wo = prepare(place, w_query[0], w_keyval[0].T, w_out[0], gain)
    kv_t = parked_keyval[0].transpose(0, 2, 1)
    stash_1 = mirror_perm(kv_t, lambda i: to_group(i, 0))
    stash_2 = mirror_perm(kv_t, lambda i: to_group(i, 1))
    stash_q = mirror_perm(parked_query[0])
    u_own = mirror_perm(parked_rows[0])
    u_z = mirror_perm(parked_rows[0], lambda i: i ^ 2)
    pieces = near + [swap_core(p) for p in near]
    u_piece = jnp.concatenate([u_own[0], u_z[0], u_own[1], u_z[1]], axis=1)
    u_piece, stash_1, stash_2, _ = tie(u_piece, stash_1, stash_2, token(pieces[7]))
    u_near = gather_y(u_piece)
    us = u_near + [swap_core(p) for p in u_near]
    stash = [stash_q, stash_1, stash_2, swap_core(stash_1), swap_core(stash_2)]

    evicted = []
    half = (SEQ, 2048)
    square = (SEQ, HD)
    for tick in range(2):
        left = [part((SEQ, 512), 0, 0)] * 8
        right = [part((SEQ, 512), 0, 1)] * 8
        q, kv, ev = call(
            qkv_body,
            pieces + [wqkv],
            left + [whole((D, 384))],
            [((SEQ, HB), BF), ((SEQ, 64), BF), ((576, HD), BF)],
            flops=2 * SEQ * D * 320,
            bytes_accessed=4 << 20,
        )
        evicted.append(ev)
        kv_mine = tp_perm(kv_pairs(kv), to_group)
        dq, dkv_mine, dkv_send = call(
            back_body,
            [place] + pieces + [wo] + stash,
            [SMEM]
            + right
            + [whole((HB, D)), part((1, SEQ, HB), tick, 0, 0)]
            + [part((1, 64, SEQ), tick, 0, 0)] * 4,
            [((SEQ, HB), BF), (square, F32), (square, BF)],
            flops=2 * SEQ * D * HB * 3,
            bytes_accessed=8 << 20,
        )
        dkv_part = tp_perm(
            (dkv_mine + swap_core(dkv_send).astype(F32)).astype(BF), from_group
        )
        dkv_part, kv_mine = tie(dkv_part, kv_mine)
        kv_other = swap_core(kv_mine)
        dkv_other = swap_core(dkv_part)
        f_keep, f_send = call(
            attend_body,
            [place, q, kv_mine, kv_other, wo],
            [SMEM, whole((SEQ, HB)), whole(square), whole(square), whole((HB, D))],
            [(half, BF), (half, BF)],
            flops=2 * SEQ * D * HB * 2,
            bytes_accessed=6 << 20,
        )
        f_got = swap_core(f_send)
        b_keep, b_send, s, inv = call(
            dnormed_body,
            [place, dq, dkv_part, dkv_other, wqkv] + us,
            [SMEM, whole((SEQ, HB)), whole(square), whole(square), whole((D, 384))]
            + [part((SEQ, 512), 0, tick)] * 8,
            [(half, BF), ((SEQ, 2176), BF), ((SEQ, 128), F32), ((SEQ, 128), F32)],
            flops=2 * SEQ * D * 320,
            bytes_accessed=6 << 20,
        )
        b_got = swap_core(b_send)
        acc, s, *sends = call(
            sum_core_body,
            [f_keep, f_got, b_keep, b_got, s],
            [whole(half), whole(half), whole(half), whole((SEQ, 2176)), whole((SEQ, 128))],
            [((SEQ, 1024), F32), ((SEQ, 128), F32)] + [((1040, 128), BF)] * 3,
        )
        gots = [swap_y(v, j + 1) for j, v in enumerate(sends)]
        if tick == 1:
            evicted[0], evicted[1], acc = tie(*evicted, acc)
            evicted = [mirror_perm(v) for v in evicted]
            evicted[0], evicted[1], gots[2] = tie(*evicted, gots[2])
        sum_ins = [acc, s] + gots + [piece, us[0], inv]
        sum_specs = (
            [whole((SEQ, 1024)), whole((SEQ, 128))]
            + [whole((1040, 128))] * 3
            + [whole((SEQ, 1024)), part((SEQ, 512), 0, tick), whole((SEQ, 128))]
        )
        if tick == 0:
            a, b = call(
                sum_y_mid_body, sum_ins, sum_specs, [((SEQ, 512), BF), ((SEQ, 512), BF)]
            )
            a_cross, b_cross = near_perm(a, 1, lambda i: i ^ 2), near_perm(b, -1, lambda i: i ^ 2)
            a, b = near_perm(a, 1), near_perm(b, -1)
            (piece,) = call(
                join_body,
                [place, a, a_cross, b, b_cross],
                [SMEM] + [whole((SEQ, 512))] * 4,
                [((SEQ, 1024), BF)],
            )
            near = gather_y(piece)
            pieces = near + [swap_core(p) for p in near]
        else:
            keep, send = call(
                sum_y_last_body, sum_ins, sum_specs, [((SEQ, 512), F32), ((SEQ, 512), BF)]
            )
            fwd_out, grad_out, out_rows, out_query, out_keyval = call(
                finish_body,
                [keep, swap_z(send)] + evicted,
                [whole((SEQ, 512))] * 2 + [whole((576, HD))] * 2,
                [
                    ((SEQ, HB), BF),
                    ((SEQ, HB), BF),
                    ((2, SEQ, HB), BF),
                    ((2, SEQ, HB), BF),
                    ((2, 64, SEQ), BF),
                ],
            )
    return (
        fwd_out[None],
        grad_out[None],
        out_rows[None],
        out_query[None],
        out_keyval.transpose(0, 2, 1)[None],
    )


def solution(mesh):
    placed = (
        P("section", None, "tp"),
        P("section", None, "tp"),
        P("section", None, None, "tp"),
        P("section", None, None, "tp"),
        P("section", None, None, "tp"),
        P("section", None),
        P("section", None, "tp"),
        P("section", None, "tp"),
        P("section", "tp", None),
    )
    return jax.shard_map(
        local,
        mesh=mesh,
        in_specs=placed,
        out_specs=(
            P("section", None, "tp"),
            P("section", None, "tp"),
            P("section", None, None, "tp"),
            P("section", None, None, "tp"),
            P("section", None, None, "tp"),
        ),
        check_vma=False,
    )
```

```python
import jax
import jax.numpy as jnp
from jax import lax
from jax.experimental import pallas as pl
from jax.experimental.pallas import tpu as pltpu
from jax.sharding import PartitionSpec as P

HD = 128
EPS = 1e-05
BF = jnp.bfloat16
F32 = jnp.float32
HB = 256
SEQ = 128
D = 4096


def tp_perm(x, f):
    return lax.ppermute(x, "tp", [(t, f(t)) for t in range(16)])


def mirror_perm(x, f=lambda t: t):
    pairs = [(s * 16 + t, (15 - s) * 16 + f(t)) for s in range(16) for t in range(16)]
    return lax.ppermute(x, ("section", "tp"), pairs)


def swap_core(x):
    return tp_perm(x, lambda t: t ^ 1)


def swap_z(x):
    return tp_perm(x, lambda t: t ^ 2)


def swap_y(x, j):
    return tp_perm(x, lambda t: t ^ (4 * j))


def near_perm(x, step, f=lambda t: t):
    pairs = [(s * 16 + t, (s + step) % 16 * 16 + f(t)) for s in range(16) for t in range(16)]
    return lax.ppermute(x, ("section", "tp"), pairs)


def to_group(t, cross=0):
    y, z, c = t // 4, t // 2 % 2, t % 2
    return (2 * (y % 2) + z) * 4 + (c ^ cross) * 2 + y // 2


def from_group(t):
    y, z, c = t // 4, t // 2 % 2, t % 2
    return (2 * c + y // 2) * 4 + (y % 2) * 2 + z


def nt(a, b):
    return lax.dot_general(a, b, (((1,), (1,)), ((), ())), preferred_element_type=F32)


def tn(a, b):
    return lax.dot_general(a, b, (((0,), (0,)), ((), ())), preferred_element_type=F32)


def nn(a, b):
    return jnp.dot(a, b, preferred_element_type=F32)


def whole(shape):
    return pl.BlockSpec(shape, lambda _: (0,) * len(shape))


def part(shape, *index):
    return pl.BlockSpec(shape, lambda _: index)


SMEM = pl.BlockSpec(memory_space=pltpu.SMEM)


def call(body, ins, specs, outs, flops=0, bytes_accessed=2 << 20):
    return pl.pallas_call(
        body,
        grid=(1,),
        in_specs=specs,
        out_specs=[whole(s) for s, _ in outs],
        out_shape=[jax.ShapeDtypeStruct(s, d) for s, d in outs],
        cost_estimate=pl.CostEstimate(
            flops=flops, bytes_accessed=bytes_accessed, transcendentals=0
        ),
        compiler_params=pltpu.CompilerParams(vmem_limit_bytes=20 << 20),
    )(*ins)


def prep_body(place, wq, wkv, wo, gain, wqkv_out, wo_out):
    column = jnp.transpose(jnp.broadcast_to(gain[...], (128, HB)))
    wide = jnp.concatenate([column, column], axis=1)
    wqkv_out[:, :HB] = (wq[...].astype(F32) * wide).astype(BF)
    tall = jnp.concatenate([wkv[...], wkv[...]], axis=0).astype(F32)
    wqkv_out[:, HB:] = (jnp.transpose(tall) * column).astype(BF)
    wo_out[...] = wo[...]


def prepare(place, wq, wkv, wo, gain):
    return pl.pallas_call(
        prep_body,
        grid_spec=pltpu.PrefetchScalarGridSpec(
            num_scalar_prefetch=1,
            grid=(16,),
            in_specs=[
                pl.BlockSpec((HB, HB), lambda k, o: (o[k], 0)),
                pl.BlockSpec((64, HB), lambda k, o: (0, o[k])),
                pl.BlockSpec((HB, HB), lambda k, o: (0, o[k])),
                pl.BlockSpec((1, HB), lambda k, o: (0, o[k])),
            ],
            out_specs=[
                pl.BlockSpec((HB, 384), lambda k, o: (k, 0)),
                pl.BlockSpec((HB, HB), lambda k, o: (0, k)),
            ],
        ),
        out_shape=[jax.ShapeDtypeStruct((D, 384), BF), jax.ShapeDtypeStruct((HB, D), BF)],
        cost_estimate=pl.CostEstimate(flops=1 << 20, bytes_accessed=10 << 20, transcendentals=0),
        compiler_params=pltpu.CompilerParams(vmem_limit_bytes=8 << 20),
    )(place, wq, wkv, wo, gain)


def pick(flag, a, b):
    return jnp.where(flag == 0, a, b)


def softmax_causal(scores):
    scores = scores * HD**-0.5
    row = lax.broadcasted_iota(jnp.int32, scores.shape, 0)
    col = lax.broadcasted_iota(jnp.int32, scores.shape, 1)
    scores = jnp.where(row >= col, scores, -1e30)
    w = jnp.exp(scores - jnp.max(scores, axis=-1, keepdims=True))
    return w / jnp.sum(w, axis=-1, keepdims=True)


def qkv_body(*refs):
    xs, w, q_out, kv_out, ev_out = refs[:8], refs[8], refs[9], refs[10], refs[11]
    acc = jnp.zeros((SEQ, 384), F32)
    squares = jnp.zeros((SEQ, 512), F32)
    for i, x in enumerate(xs):
        xv = x[...]
        xf = xv.astype(F32)
        squares = squares + xf * xf
        acc = acc + nn(xv, w[512 * i : 512 * i + 512, :])
    inv = lax.rsqrt(jnp.sum(squares, axis=-1, keepdims=True) * (1.0 / D) + EPS)
    out = acc * inv
    q_out[...] = out[:, :HB].astype(BF)
    kv_out[...] = out[:, HB : HB + 64].astype(BF)
    ev_out[:SEQ, :] = out[:, :HD].astype(BF)
    ev_out[SEQ : 2 * SEQ, :] = out[:, HD:HB].astype(BF)
    ev_out[2 * SEQ : 3 * SEQ, :] = xs[0][:, :HD]
    ev_out[3 * SEQ : 4 * SEQ, :] = xs[0][:, HD : 2 * HD]
    ev_out[4 * SEQ :, :] = jnp.transpose(out[:, HB:])[:64, :].astype(BF)


def back_body(place, *refs):
    gs, wo, sq, m1, m2, o1, o2 = refs[:8], *refs[8:14]
    dq_out, mine_out, send_out = refs[14:]
    core, z = place[16], place[17]
    acc = jnp.zeros((SEQ, HB), F32)
    for i, g in enumerate(gs):
        acc = acc + nt(g[...], wo[:, 512 * i : 512 * i + 512])
    hg = acc.astype(BF)

    def joined(a, b):
        return jnp.concatenate([pick(z, a[0], b[0]), pick(z, b[0], a[0])], axis=0)

    mine, other = joined(m1, m2), joined(o1, o2)
    key_t, val_t = pick(core, mine, other), pick(core, other, mine)
    dk = jnp.zeros((SEQ, HD), F32)
    dv = jnp.zeros((SEQ, HD), F32)
    for h in range(2):
        cut = slice(h * HD, h * HD + HD)
        q = sq[0][:, cut]
        hgh = hg[:, cut]
        p = softmax_causal(nn(q, key_t))
        dp = nn(hgh, val_t)
        delta = jnp.sum(dp * p, axis=-1, keepdims=True)
        ds = (p * (dp - delta) * HD**-0.5).astype(BF)
        dq_out[:, cut] = nt(ds, key_t).astype(BF)
        dk = dk + tn(ds, q)
        dv = dv + tn(p.astype(BF), hgh)
    mine_out[...] = pick(core, dk, dv)
    send_out[...] = pick(core, dv, dk).astype(BF)


def attend_body(place, q, kv_mine, kv_other, wo, keep_out, send_out):
    core = place[16]
    mine, other = kv_mine[...], kv_other[...]
    key, val = pick(core, mine, other), pick(core, other, mine)
    heads = []
    for h in range(2):
        p = softmax_causal(nt(q[:, h * HD : h * HD + HD], key))
        heads.append(nn(p.astype(BF), val))
    mixed = jnp.concatenate(heads, axis=1).astype(BF)
    for i in range(4):
        cut = slice(512 * i, 512 * i + 512)
        send_out[:, cut] = nn(mixed, wo[:, 2048 + 512 * i : 2560 + 512 * i]).astype(BF)
        keep_out[:, cut] = nn(mixed, wo[:, cut]).astype(BF)


def dnormed_body(place, dq, part_mine, part_other, w, *refs):
    us, keep_out, send_out, s_out, inv_out = refs[:8], refs[8], refs[9], refs[10], refs[11]
    both = part_mine[...].astype(F32) + part_other[...].astype(F32)
    lane = lax.broadcasted_iota(jnp.int32, both.shape, 1)
    dkv = jnp.where(lane // 64 == place[16], both, 0.0).astype(BF)
    d = jnp.concatenate([dq[...], dkv], axis=1)
    dots = jnp.zeros((SEQ, 512), F32)
    squares = jnp.zeros((SEQ, 512), F32)
    for i in range(8):
        dn = nt(d, w[512 * i : 512 * i + 512, :])
        u = us[i][...].astype(F32)
        dots = dots + dn * u
        squares = squares + u * u
        if i < 4:
            keep_out[:, 512 * i : 512 * i + 512] = dn.astype(BF)
        else:
            send_out[:, 512 * i - 2048 : 512 * i - 1536] = dn.astype(BF)
    inv = lax.rsqrt(jnp.sum(squares, axis=-1, keepdims=True) * (1.0 / D) + EPS)
    s = jnp.sum(dots, axis=-1, keepdims=True) * inv
    send_out[:, 2048:] = spread(s)
    s_out[...] = jnp.broadcast_to(s, (SEQ, 128))
    inv_out[...] = jnp.broadcast_to(inv, (SEQ, 128))


def spread(s):
    hi = s.astype(BF).astype(F32)
    lane = lax.broadcasted_iota(jnp.int32, (SEQ, 128), 1)
    return jnp.where(lane == 0, hi, jnp.where(lane == 1, s - hi, 0.0)).astype(BF)


def total(block):
    b = block.astype(F32)
    return b[:, 0:1] + b[:, 1:2]


def sum_core_body(f_keep, f_got, b_keep, b_got, s_in, acc_out, s_out, *sends):
    s = s_in[...][:, 0:1] + total(b_got[:, 2048:])
    wide = jnp.broadcast_to(s, (SEQ, 128))
    s_out[...] = wide
    flat = jnp.transpose(wide)[:16, :]
    hi = flat.astype(BF).astype(F32)
    row = lax.broadcasted_iota(jnp.int32, (16, 128), 0)
    flat = jnp.where(row < 8, hi, flat - hi).astype(BF)
    for j in range(4):
        cut = slice(512 * j, 512 * j + 512)
        f = f_keep[:, cut].astype(F32) + f_got[:, cut].astype(F32)
        b = b_keep[:, cut].astype(F32) + b_got[:, cut].astype(F32)
        if j == 0:
            acc_out[:, :512] = f
            acc_out[:, 512:] = b
        else:
            for i in range(4):
                sub = slice(128 * i, 128 * i + 128)
                sends[j - 1][128 * i : 128 * i + 128, :] = f[:, sub].astype(BF)
                sends[j - 1][512 + 128 * i : 640 + 128 * i, :] = b[:, sub].astype(BF)
            sends[j - 1][1024:, :] = flat


def sum_y(acc, s_in, gots, xg, u, inv_in):
    tot = []
    for i in range(8):
        sub = slice(128 * i, 128 * i + 128)
        v = acc[:, sub]
        for got in gots:
            v = v + got[sub, :].astype(F32)
        tot.append(v)
    flat = jnp.zeros((1, 128), F32)
    for got in gots:
        low = got[1024:, :].astype(F32)
        flat = flat + low[0:1, :] + low[8:9, :]
    s = s_in[...] + jnp.transpose(jnp.broadcast_to(flat, (128, 128)))
    inv = inv_in[...]
    mean = s * inv * (1.0 / D)
    for i in range(4):
        sub = slice(128 * i, 128 * i + 128)
        back = inv * (tot[4 + i] - u[:, sub].astype(F32) * mean)
        if i < 2:
            tot[i] = tot[i] + xg[:, sub].astype(F32)
            back = back + xg[:, 512 + 128 * i : 640 + 128 * i].astype(F32)
        tot[4 + i] = back
    return tot


def sum_y_mid_body(acc, s_in, g1, g2, g3, xg, u, inv_in, a_out, b_out):
    tot = sum_y(acc, s_in, (g1, g2, g3), xg, u, inv_in)
    for i in range(4):
        a_out[:, 128 * i : 128 * i + 128] = tot[i].astype(BF)
        b_out[:, 128 * i : 128 * i + 128] = tot[4 + i].astype(BF)


def sum_y_last_body(acc, s_in, g1, g2, g3, xg, u, inv_in, keep_out, send_out):
    tot = sum_y(acc, s_in, (g1, g2, g3), xg, u, inv_in)
    for i in range(2):
        sub = slice(128 * i, 128 * i + 128)
        far = slice(HB + 128 * i, HB + 128 * i + 128)
        keep_out[:, sub] = tot[i]
        keep_out[:, far] = tot[4 + i]
        send_out[:, sub] = tot[2 + i].astype(BF)
        send_out[:, far] = tot[6 + i].astype(BF)


def join_body(place, a, a_cross, b, b_cross, out):
    for at, same, cross, edge in ((0, a, a_cross, 0), (512, b, b_cross, 15)):
        for lo, hi in ((0, HB), (HB, 0)):
            v = same[:, lo : lo + HB].astype(F32) + cross[:, hi : hi + HB].astype(F32)
            v = jnp.where(place[18] == edge, 0.0, v)
            out[:, at + lo : at + lo + HB] = v.astype(BF)


def finish_body(keep, got, ev0, ev1, f_out, g_out, rows_out, query_out, keyval_out):
    f_out[...] = (keep[:, :HB] + got[:, :HB].astype(F32)).astype(BF)
    g_out[...] = (keep[:, HB:] + got[:, HB:].astype(F32)).astype(BF)
    for i, ev in enumerate((ev0, ev1)):
        query_out[i, :, :HD] = ev[:SEQ, :]
        query_out[i, :, HD:] = ev[SEQ : 2 * SEQ, :]
        rows_out[i, :, :HD] = ev[2 * SEQ : 3 * SEQ, :]
        rows_out[i, :, HD:] = ev[3 * SEQ : 4 * SEQ, :]
        keyval_out[i, :, :] = ev[4 * SEQ :, :]


def gather_y(piece):
    return [piece] + [swap_y(piece, j) for j in (1, 2, 3)]


def tie(*values):
    return list(lax.optimization_barrier(values))


def local(
    fwd_in, grad_in, parked_rows, parked_query, parked_keyval, norm_gain, w_query, w_keyval, w_out
):
    t = lax.axis_index("tp").astype(jnp.int32)
    ks = jnp.array(
        [ky * 4 + kz * 2 + kc for kc in range(2) for ky in range(4) for kz in range(2)], jnp.int32
    )
    section = lax.axis_index("section").astype(jnp.int32)
    place = jnp.concatenate([jnp.bitwise_xor(ks, t), jnp.stack([t % 2, t // 2 % 2, section])])
    core = t % 2

    def kv_pairs(kv):
        other = swap_core(kv)
        return pick(
            core,
            jnp.concatenate([kv, other], axis=-1),
            jnp.concatenate([other, kv], axis=-1),
        )

    def token(v):
        return v[:8, :128]

    x, g = fwd_in[0], grad_in[0]
    xg_z = swap_z(jnp.concatenate([x, g], axis=1))
    piece = jnp.concatenate([x, xg_z[:, :HB], g, xg_z[:, HB:]], axis=1)
    near = gather_y(piece)
    gain, _ = tie(norm_gain, token(piece))
    wqkv, wo = prepare(place, w_query[0], w_keyval[0].T, w_out[0], gain)
    kv_t = parked_keyval[0].transpose(0, 2, 1)
    stash_1 = mirror_perm(kv_t, lambda i: to_group(i, 0))
    stash_2 = mirror_perm(kv_t, lambda i: to_group(i, 1))
    stash_q = mirror_perm(parked_query[0])
    u_own = mirror_perm(parked_rows[0])
    u_z = mirror_perm(parked_rows[0], lambda i: i ^ 2)
    pieces = near + [swap_core(p) for p in near]
    u_piece = jnp.concatenate([u_own[0], u_z[0], u_own[1], u_z[1]], axis=1)
    u_piece, stash_1, stash_2, _ = tie(u_piece, stash_1, stash_2, token(pieces[7]))
    u_near = gather_y(u_piece)
    us = u_near + [swap_core(p) for p in u_near]
    stash = [stash_q, stash_1, stash_2, swap_core(stash_1), swap_core(stash_2)]

    evicted = []
    half = (SEQ, 2048)
    square = (SEQ, HD)
    for tick in range(2):
        left = [part((SEQ, 512), 0, 0)] * 8
        right = [part((SEQ, 512), 0, 1)] * 8
        q, kv, ev = call(
            qkv_body,
            pieces + [wqkv],
            left + [whole((D, 384))],
            [((SEQ, HB), BF), ((SEQ, 64), BF), ((576, HD), BF)],
            flops=2 * SEQ * D * 320,
            bytes_accessed=4 << 20,
        )
        evicted.append(ev)
        kv_mine = tp_perm(kv_pairs(kv), to_group)
        dq, dkv_mine, dkv_send = call(
            back_body,
            [place] + pieces + [wo] + stash,
            [SMEM]
            + right
            + [whole((HB, D)), part((1, SEQ, HB), tick, 0, 0)]
            + [part((1, 64, SEQ), tick, 0, 0)] * 4,
            [((SEQ, HB), BF), (square, F32), (square, BF)],
            flops=2 * SEQ * D * HB * 3,
            bytes_accessed=8 << 20,
        )
        dkv_part = tp_perm(
            (dkv_mine + swap_core(dkv_send).astype(F32)).astype(BF), from_group
        )
        dkv_part, kv_mine = tie(dkv_part, kv_mine)
        kv_other = swap_core(kv_mine)
        dkv_other = swap_core(dkv_part)
        f_keep, f_send = call(
            attend_body,
            [place, q, kv_mine, kv_other, wo],
            [SMEM, whole((SEQ, HB)), whole(square), whole(square), whole((HB, D))],
            [(half, BF), (half, BF)],
            flops=2 * SEQ * D * HB * 2,
            bytes_accessed=6 << 20,
        )
        f_got = swap_core(f_send)
        b_keep, b_send, s, inv = call(
            dnormed_body,
            [place, dq, dkv_part, dkv_other, wqkv] + us,
            [SMEM, whole((SEQ, HB)), whole(square), whole(square), whole((D, 384))]
            + [part((SEQ, 512), 0, tick)] * 8,
            [(half, BF), ((SEQ, 2176), BF), ((SEQ, 128), F32), ((SEQ, 128), F32)],
            flops=2 * SEQ * D * 320,
            bytes_accessed=6 << 20,
        )
        b_got = swap_core(b_send)
        acc, s, *sends = call(
            sum_core_body,
            [f_keep, f_got, b_keep, b_got, s],
            [whole(half), whole(half), whole(half), whole((SEQ, 2176)), whole((SEQ, 128))],
            [((SEQ, 1024), F32), ((SEQ, 128), F32)] + [((1040, 128), BF)] * 3,
        )
        gots = [swap_y(v, j + 1) for j, v in enumerate(sends)]
        if tick == 1:
            evicted[0], evicted[1], acc = tie(*evicted, acc)
            evicted = [mirror_perm(v) for v in evicted]
            evicted[0], evicted[1], gots[2] = tie(*evicted, gots[2])
        sum_ins = [acc, s] + gots + [piece, us[0], inv]
        sum_specs = (
            [whole((SEQ, 1024)), whole((SEQ, 128))]
            + [whole((1040, 128))] * 3
            + [whole((SEQ, 1024)), part((SEQ, 512), 0, tick), whole((SEQ, 128))]
        )
        if tick == 0:
            a, b = call(
                sum_y_mid_body, sum_ins, sum_specs, [((SEQ, 512), BF), ((SEQ, 512), BF)]
            )
            a_cross, b_cross = near_perm(a, 1, lambda i: i ^ 2), near_perm(b, -1, lambda i: i ^ 2)
            a, b = near_perm(a, 1), near_perm(b, -1)
            (piece,) = call(
                join_body,
                [place, a, a_cross, b, b_cross],
                [SMEM] + [whole((SEQ, 512))] * 4,
                [((SEQ, 1024), BF)],
            )
            near = gather_y(piece)
            pieces = near + [swap_core(p) for p in near]
        else:
            keep, send = call(
                sum_y_last_body, sum_ins, sum_specs, [((SEQ, 512), F32), ((SEQ, 512), BF)]
            )
            fwd_out, grad_out, out_rows, out_query, out_keyval = call(
                finish_body,
                [keep, swap_z(send)] + evicted,
                [whole((SEQ, 512))] * 2 + [whole((576, HD))] * 2,
                [
                    ((SEQ, HB), BF),
                    ((SEQ, HB), BF),
                    ((2, SEQ, HB), BF),
                    ((2, SEQ, HB), BF),
                    ((2, 64, SEQ), BF),
                ],
            )
    return (
        fwd_out[None],
        grad_out[None],
        out_rows[None],
        out_query[None],
        out_keyval.transpose(0, 2, 1)[None],
    )


def solution(mesh):
    placed = (
        P("section", None, "tp"),
        P("section", None, "tp"),
        P("section", None, None, "tp"),
        P("section", None, None, "tp"),
        P("section", None, None, "tp"),
        P("section", None),
        P("section", None, "tp"),
        P("section", None, "tp"),
        P("section", "tp", None),
    )
    return jax.shard_map(
        local,
        mesh=mesh,
        in_specs=placed,
        out_specs=(
            P("section", None, "tp"),
            P("section", None, "tp"),
            P("section", None, None, "tp"),
            P("section", None, None, "tp"),
            P("section", None, None, "tp"),
        ),
        check_vma=False,
    )
```

```python
import jax
import jax.numpy as jnp
from jax import lax
from jax.experimental import pallas as pl
from jax.experimental.pallas import tpu as pltpu
from jax.sharding import PartitionSpec as P

HD = 128
EPS = 1e-05
BF = jnp.bfloat16
F32 = jnp.float32
HB = 256
SEQ = 128
D = 4096


def tp_perm(x, f):
    return lax.ppermute(x, "tp", [(t, f(t)) for t in range(16)])


def mirror_perm(x, f=lambda t: t):
    pairs = [(s * 16 + t, (15 - s) * 16 + f(t)) for s in range(16) for t in range(16)]
    return lax.ppermute(x, ("section", "tp"), pairs)


def swap_core(x):
    return tp_perm(x, lambda t: t ^ 1)


def swap_z(x):
    return tp_perm(x, lambda t: t ^ 2)


def swap_y(x, j):
    return tp_perm(x, lambda t: t ^ (4 * j))


def near_perm(x, step, f=lambda t: t):
    pairs = [(s * 16 + t, (s + step) % 16 * 16 + f(t)) for s in range(16) for t in range(16)]
    return lax.ppermute(x, ("section", "tp"), pairs)


def to_group(t, cross=0):
    y, z, c = t // 4, t // 2 % 2, t % 2
    return (2 * (y % 2) + z) * 4 + (c ^ cross) * 2 + y // 2


def from_group(t):
    y, z, c = t // 4, t // 2 % 2, t % 2
    return (2 * c + y // 2) * 4 + (y % 2) * 2 + z


def nt(a, b):
    return lax.dot_general(a, b, (((1,), (1,)), ((), ())), preferred_element_type=F32)


def tn(a, b):
    return lax.dot_general(a, b, (((0,), (0,)), ((), ())), preferred_element_type=F32)


def nn(a, b):
    return jnp.dot(a, b, preferred_element_type=F32)


def whole(shape):
    return pl.BlockSpec(shape, lambda _: (0,) * len(shape))


def part(shape, *index):
    return pl.BlockSpec(shape, lambda _: index)


SMEM = pl.BlockSpec(memory_space=pltpu.SMEM)


def call(body, ins, specs, outs, flops=0, bytes_accessed=2 << 20):
    return pl.pallas_call(
        body,
        grid=(1,),
        in_specs=specs,
        out_specs=[whole(s) for s, _ in outs],
        out_shape=[jax.ShapeDtypeStruct(s, d) for s, d in outs],
        cost_estimate=pl.CostEstimate(
            flops=flops, bytes_accessed=bytes_accessed, transcendentals=0
        ),
        compiler_params=pltpu.CompilerParams(vmem_limit_bytes=20 << 20),
    )(*ins)


def prep_body(place, wq, wkv, wo, gain, wqkv_out, wo_out):
    column = jnp.transpose(jnp.broadcast_to(gain[...], (128, HB)))
    wide = jnp.concatenate([column, column], axis=1)
    wqkv_out[:, :HB] = (wq[...].astype(F32) * wide).astype(BF)
    tall = jnp.concatenate([wkv[...], wkv[...]], axis=0).astype(F32)
    wqkv_out[:, HB:] = (jnp.transpose(tall) * column).astype(BF)
    wo_out[...] = wo[...]


def prepare(place, wq, wkv, wo, gain):
    return pl.pallas_call(
        prep_body,
        grid_spec=pltpu.PrefetchScalarGridSpec(
            num_scalar_prefetch=1,
            grid=(16,),
            in_specs=[
                pl.BlockSpec((HB, HB), lambda k, o: (o[k], 0)),
                pl.BlockSpec((64, HB), lambda k, o: (0, o[k])),
                pl.BlockSpec((HB, HB), lambda k, o: (0, o[k])),
                pl.BlockSpec((1, HB), lambda k, o: (0, o[k])),
            ],
            out_specs=[
                pl.BlockSpec((HB, 384), lambda k, o: (k, 0)),
                pl.BlockSpec((HB, HB), lambda k, o: (0, k)),
            ],
        ),
        out_shape=[jax.ShapeDtypeStruct((D, 384), BF), jax.ShapeDtypeStruct((HB, D), BF)],
        cost_estimate=pl.CostEstimate(flops=1 << 20, bytes_accessed=10 << 20, transcendentals=0),
        compiler_params=pltpu.CompilerParams(vmem_limit_bytes=8 << 20),
    )(place, wq, wkv, wo, gain)


def pick(flag, a, b):
    return jnp.where(flag == 0, a, b)


def softmax_causal(scores):
    scores = scores * HD**-0.5
    row = lax.broadcasted_iota(jnp.int32, scores.shape, 0)
    col = lax.broadcasted_iota(jnp.int32, scores.shape, 1)
    scores = jnp.where(row >= col, scores, -1e30)
    w = jnp.exp(scores - jnp.max(scores, axis=-1, keepdims=True))
    return w / jnp.sum(w, axis=-1, keepdims=True)


def qkv_body(*refs):
    xs, w, q_out, kv_out, ev_out = refs[:8], refs[8], refs[9], refs[10], refs[11]
    acc = jnp.zeros((SEQ, 384), F32)
    squares = jnp.zeros((SEQ, 512), F32)
    for i, x in enumerate(xs):
        xv = x[...]
        xf = xv.astype(F32)
        squares = squares + xf * xf
        acc = acc + nn(xv, w[512 * i : 512 * i + 512, :])
    inv = lax.rsqrt(jnp.sum(squares, axis=-1, keepdims=True) * (1.0 / D) + EPS)
    out = acc * inv
    q_out[...] = out[:, :HB].astype(BF)
    kv_out[...] = out[:, HB : HB + 64].astype(BF)
    ev_out[:SEQ, :] = out[:, :HD].astype(BF)
    ev_out[SEQ : 2 * SEQ, :] = out[:, HD:HB].astype(BF)
    ev_out[2 * SEQ : 3 * SEQ, :] = xs[0][:, :HD]
    ev_out[3 * SEQ : 4 * SEQ, :] = xs[0][:, HD : 2 * HD]
    ev_out[4 * SEQ :, :] = jnp.transpose(out[:, HB:])[:64, :].astype(BF)


def back_body(place, *refs):
    gs, wo, sq, m1, m2, o1, o2 = refs[:8], *refs[8:14]
    dq_out, mine_out, send_out = refs[14:]
    core, z = place[16], place[17]
    acc = jnp.zeros((SEQ, HB), F32)
    for i, g in enumerate(gs):
        acc = acc + nt(g[...], wo[:, 512 * i : 512 * i + 512])
    hg = acc.astype(BF)

    def joined(a, b):
        return jnp.concatenate([pick(z, a[0], b[0]), pick(z, b[0], a[0])], axis=0)

    mine, other = joined(m1, m2), joined(o1, o2)
    key_t, val_t = pick(core, mine, other), pick(core, other, mine)
    dk = jnp.zeros((SEQ, HD), F32)
    dv = jnp.zeros((SEQ, HD), F32)
    for h in range(2):
        cut = slice(h * HD, h * HD + HD)
        q = sq[0][:, cut]
        hgh = hg[:, cut]
        p = softmax_causal(nn(q, key_t))
        dp = nn(hgh, val_t)
        delta = jnp.sum(dp * p, axis=-1, keepdims=True)
        ds = (p * (dp - delta) * HD**-0.5).astype(BF)
        dq_out[:, cut] = nt(ds, key_t).astype(BF)
        dk = dk + tn(ds, q)
        dv = dv + tn(p.astype(BF), hgh)
    mine_out[...] = pick(core, dk, dv)
    send_out[...] = pick(core, dv, dk).astype(BF)


def attend_body(place, q, kv_mine, kv_other, wo, keep_out, send_out):
    core = place[16]
    mine, other = kv_mine[...], kv_other[...]
    key, val = pick(core, mine, other), pick(core, other, mine)
    heads = []
    for h in range(2):
        p = softmax_causal(nt(q[:, h * HD : h * HD + HD], key))
        heads.append(nn(p.astype(BF), val))
    mixed = jnp.concatenate(heads, axis=1).astype(BF)
    for i in range(4):
        cut = slice(512 * i, 512 * i + 512)
        send_out[:, cut] = nn(mixed, wo[:, 2048 + 512 * i : 2560 + 512 * i]).astype(BF)
        keep_out[:, cut] = nn(mixed, wo[:, cut]).astype(BF)


def dnormed_body(place, dq, part_mine, part_other, w, *refs):
    us, keep_out, send_out, s_out, inv_out = refs[:8], refs[8], refs[9], refs[10], refs[11]
    both = part_mine[...].astype(F32) + part_other[...].astype(F32)
    lane = lax.broadcasted_iota(jnp.int32, both.shape, 1)
    dkv = jnp.where(lane // 64 == place[16], both, 0.0).astype(BF)
    d = jnp.concatenate([dq[...], dkv], axis=1)
    dots = jnp.zeros((SEQ, 512), F32)
    squares = jnp.zeros((SEQ, 512), F32)
    for i in range(8):
        dn = nt(d, w[512 * i : 512 * i + 512, :])
        u = us[i][...].astype(F32)
        dots = dots + dn * u
        squares = squares + u * u
        if i < 4:
            keep_out[:, 512 * i : 512 * i + 512] = dn.astype(BF)
        else:
            send_out[:, 512 * i - 2048 : 512 * i - 1536] = dn.astype(BF)
    inv = lax.rsqrt(jnp.sum(squares, axis=-1, keepdims=True) * (1.0 / D) + EPS)
    s = jnp.sum(dots, axis=-1, keepdims=True) * inv
    send_out[:, 2048:] = spread(s)
    s_out[...] = jnp.broadcast_to(s, (SEQ, 128))
    inv_out[...] = jnp.broadcast_to(inv, (SEQ, 128))


def spread(s):
    hi = s.astype(BF).astype(F32)
    lane = lax.broadcasted_iota(jnp.int32, (SEQ, 128), 1)
    return jnp.where(lane == 0, hi, jnp.where(lane == 1, s - hi, 0.0)).astype(BF)


def total(block):
    b = block.astype(F32)
    return b[:, 0:1] + b[:, 1:2]


def sum_core_body(f_keep, f_got, b_keep, b_got, s_in, acc_out, s_out, *sends):
    s = s_in[...][:, 0:1] + total(b_got[:, 2048:])
    wide = jnp.broadcast_to(s, (SEQ, 128))
    s_out[...] = wide
    flat = jnp.transpose(wide)[:16, :]
    hi = flat.astype(BF).astype(F32)
    row = lax.broadcasted_iota(jnp.int32, (16, 128), 0)
    flat = jnp.where(row < 8, hi, flat - hi).astype(BF)
    for j in range(4):
        cut = slice(512 * j, 512 * j + 512)
        f = f_keep[:, cut].astype(F32) + f_got[:, cut].astype(F32)
        b = b_keep[:, cut].astype(F32) + b_got[:, cut].astype(F32)
        if j == 0:
            acc_out[:, :512] = f
            acc_out[:, 512:] = b
        else:
            for i in range(4):
                sub = slice(128 * i, 128 * i + 128)
                sends[j - 1][128 * i : 128 * i + 128, :] = f[:, sub].astype(BF)
                sends[j - 1][512 + 128 * i : 640 + 128 * i, :] = b[:, sub].astype(BF)
            sends[j - 1][1024:, :] = flat


def sum_y(acc, s_in, gots, xg, u, inv_in):
    tot = []
    for i in range(8):
        sub = slice(128 * i, 128 * i + 128)
        v = acc[:, sub]
        for got in gots:
            v = v + got[sub, :].astype(F32)
        tot.append(v)
    flat = jnp.zeros((1, 128), F32)
    for got in gots:
        low = got[1024:, :].astype(F32)
        flat = flat + low[0:1, :] + low[8:9, :]
    s = s_in[...] + jnp.transpose(jnp.broadcast_to(flat, (128, 128)))
    inv = inv_in[...]
    mean = s * inv * (1.0 / D)
    for i in range(4):
        sub = slice(128 * i, 128 * i + 128)
        back = inv * (tot[4 + i] - u[:, sub].astype(F32) * mean)
        if i < 2:
            tot[i] = tot[i] + xg[:, sub].astype(F32)
            back = back + xg[:, 512 + 128 * i : 640 + 128 * i].astype(F32)
        tot[4 + i] = back
    return tot


def sum_y_mid_body(acc, s_in, g1, g2, g3, xg, u, inv_in, a_out, b_out):
    tot = sum_y(acc, s_in, (g1, g2, g3), xg, u, inv_in)
    for i in range(4):
        a_out[:, 128 * i : 128 * i + 128] = tot[i].astype(BF)
        b_out[:, 128 * i : 128 * i + 128] = tot[4 + i].astype(BF)


def sum_y_last_body(acc, s_in, g1, g2, g3, xg, u, inv_in, keep_out, send_out):
    tot = sum_y(acc, s_in, (g1, g2, g3), xg, u, inv_in)
    for i in range(2):
        sub = slice(128 * i, 128 * i + 128)
        far = slice(HB + 128 * i, HB + 128 * i + 128)
        keep_out[:, sub] = tot[i]
        keep_out[:, far] = tot[4 + i]
        send_out[:, sub] = tot[2 + i].astype(BF)
        send_out[:, far] = tot[6 + i].astype(BF)


def join_body(place, a, a_cross, b, b_cross, out):
    for at, same, cross, edge in ((0, a, a_cross, 0), (512, b, b_cross, 15)):
        for lo, hi in ((0, HB), (HB, 0)):
            v = same[:, lo : lo + HB].astype(F32) + cross[:, hi : hi + HB].astype(F32)
            v = jnp.where(place[18] == edge, 0.0, v)
            out[:, at + lo : at + lo + HB] = v.astype(BF)


def finish_body(keep, got, ev0, ev1, f_out, g_out, rows_out, query_out, keyval_out):
    f_out[...] = (keep[:, :HB] + got[:, :HB].astype(F32)).astype(BF)
    g_out[...] = (keep[:, HB:] + got[:, HB:].astype(F32)).astype(BF)
    for i, ev in enumerate((ev0, ev1)):
        query_out[i, :, :HD] = ev[:SEQ, :]
        query_out[i, :, HD:] = ev[SEQ : 2 * SEQ, :]
        rows_out[i, :, :HD] = ev[2 * SEQ : 3 * SEQ, :]
        rows_out[i, :, HD:] = ev[3 * SEQ : 4 * SEQ, :]
        keyval_out[i, :, :] = ev[4 * SEQ :, :]


def gather_y(piece):
    return [piece] + [swap_y(piece, j) for j in (1, 2, 3)]


def tie(*values):
    return list(lax.optimization_barrier(values))


def local(
    fwd_in, grad_in, parked_rows, parked_query, parked_keyval, norm_gain, w_query, w_keyval, w_out
):
    t = lax.axis_index("tp").astype(jnp.int32)
    ks = jnp.array(
        [ky * 4 + kz * 2 + kc for kc in range(2) for ky in range(4) for kz in range(2)], jnp.int32
    )
    section = lax.axis_index("section").astype(jnp.int32)
    place = jnp.concatenate([jnp.bitwise_xor(ks, t), jnp.stack([t % 2, t // 2 % 2, section])])
    core = t % 2

    def kv_pairs(kv):
        other = swap_core(kv)
        return pick(
            core,
            jnp.concatenate([kv, other], axis=-1),
            jnp.concatenate([other, kv], axis=-1),
        )

    def token(v):
        return v[:8, :128]

    x, g = fwd_in[0], grad_in[0]
    xg_z = swap_z(jnp.concatenate([x, g], axis=1))
    piece = jnp.concatenate([x, xg_z[:, :HB], g, xg_z[:, HB:]], axis=1)
    near = gather_y(piece)
    gain, _ = tie(norm_gain, token(piece))
    wqkv, wo = prepare(place, w_query[0], w_keyval[0].T, w_out[0], gain)
    kv_t = parked_keyval[0].transpose(0, 2, 1)
    stash_1 = mirror_perm(kv_t, lambda i: to_group(i, 0))
    stash_2 = mirror_perm(kv_t, lambda i: to_group(i, 1))
    stash_q = mirror_perm(parked_query[0])
    u_own = mirror_perm(parked_rows[0])
    u_z = mirror_perm(parked_rows[0], lambda i: i ^ 2)
    pieces = near + [swap_core(p) for p in near]
    u_piece = jnp.concatenate([u_own[0], u_z[0], u_own[1], u_z[1]], axis=1)
    u_piece, stash_1, stash_2, _ = tie(u_piece, stash_1, stash_2, token(pieces[7]))
    u_near = gather_y(u_piece)
    us = u_near + [swap_core(p) for p in u_near]
    stash = [stash_q, stash_1, stash_2, swap_core(stash_1), swap_core(stash_2)]

    evicted = []
    half = (SEQ, 2048)
    square = (SEQ, HD)
    for tick in range(2):
        left = [part((SEQ, 512), 0, 0)] * 8
        right = [part((SEQ, 512), 0, 1)] * 8
        q, kv, ev = call(
            qkv_body,
            pieces + [wqkv],
            left + [whole((D, 384))],
            [((SEQ, HB), BF), ((SEQ, 64), BF), ((576, HD), BF)],
            flops=2 * SEQ * D * 320,
            bytes_accessed=4 << 20,
        )
        evicted.append(ev)
        kv_mine = tp_perm(kv_pairs(kv), to_group)
        dq, dkv_mine, dkv_send = call(
            back_body,
            [place] + pieces + [wo] + stash,
            [SMEM]
            + right
            + [whole((HB, D)), part((1, SEQ, HB), tick, 0, 0)]
            + [part((1, 64, SEQ), tick, 0, 0)] * 4,
            [((SEQ, HB), BF), (square, F32), (square, BF)],
            flops=2 * SEQ * D * HB * 3,
            bytes_accessed=8 << 20,
        )
        dkv_part = tp_perm(
            (dkv_mine + swap_core(dkv_send).astype(F32)).astype(BF), from_group
        )
        if tick == 1:
            dkv_part, kv_mine = tie(dkv_part, kv_mine)
        kv_other = swap_core(kv_mine)
        dkv_other = swap_core(dkv_part)
        f_keep, f_send = call(
            attend_body,
            [place, q, kv_mine, kv_other, wo],
            [SMEM, whole((SEQ, HB)), whole(square), whole(square), whole((HB, D))],
            [(half, BF), (half, BF)],
            flops=2 * SEQ * D * HB * 2,
            bytes_accessed=6 << 20,
        )
        f_got = swap_core(f_send)
        b_keep, b_send, s, inv = call(
            dnormed_body,
            [place, dq, dkv_part, dkv_other, wqkv] + us,
            [SMEM, whole((SEQ, HB)), whole(square), whole(square), whole((D, 384))]
            + [part((SEQ, 512), 0, tick)] * 8,
            [(half, BF), ((SEQ, 2176), BF), ((SEQ, 128), F32), ((SEQ, 128), F32)],
            flops=2 * SEQ * D * 320,
            bytes_accessed=6 << 20,
        )
        b_got = swap_core(b_send)
        acc, s, *sends = call(
            sum_core_body,
            [f_keep, f_got, b_keep, b_got, s],
            [whole(half), whole(half), whole(half), whole((SEQ, 2176)), whole((SEQ, 128))],
            [((SEQ, 1024), F32), ((SEQ, 128), F32)] + [((1040, 128), BF)] * 3,
        )
        gots = [swap_y(v, j + 1) for j, v in enumerate(sends)]
        if tick == 1:
            evicted[0], evicted[1], acc = tie(*evicted, acc)
            evicted = [mirror_perm(v) for v in evicted]
            evicted[0], evicted[1], gots[2] = tie(*evicted, gots[2])
        sum_ins = [acc, s] + gots + [piece, us[0], inv]
        sum_specs = (
            [whole((SEQ, 1024)), whole((SEQ, 128))]
            + [whole((1040, 128))] * 3
            + [whole((SEQ, 1024)), part((SEQ, 512), 0, tick), whole((SEQ, 128))]
        )
        if tick == 0:
            a, b = call(
                sum_y_mid_body, sum_ins, sum_specs, [((SEQ, 512), BF), ((SEQ, 512), BF)]
            )
            a_cross, b_cross = near_perm(a, 1, lambda i: i ^ 2), near_perm(b, -1, lambda i: i ^ 2)
            a, b = near_perm(a, 1), near_perm(b, -1)
            (piece,) = call(
                join_body,
                [place, a, a_cross, b, b_cross],
                [SMEM] + [whole((SEQ, 512))] * 4,
                [((SEQ, 1024), BF)],
            )
            near = gather_y(piece)
            pieces = near + [swap_core(p) for p in near]
        else:
            keep, send = call(
                sum_y_last_body, sum_ins, sum_specs, [((SEQ, 512), F32), ((SEQ, 512), BF)]
            )
            fwd_out, grad_out, out_rows, out_query, out_keyval = call(
                finish_body,
                [keep, swap_z(send)] + evicted,
                [whole((SEQ, 512))] * 2 + [whole((576, HD))] * 2,
                [
                    ((SEQ, HB), BF),
                    ((SEQ, HB), BF),
                    ((2, SEQ, HB), BF),
                    ((2, SEQ, HB), BF),
                    ((2, 64, SEQ), BF),
                ],
            )
    return (
        fwd_out[None],
        grad_out[None],
        out_rows[None],
        out_query[None],
        out_keyval.transpose(0, 2, 1)[None],
    )


def solution(mesh):
    placed = (
        P("section", None, "tp"),
        P("section", None, "tp"),
        P("section", None, None, "tp"),
        P("section", None, None, "tp"),
        P("section", None, None, "tp"),
        P("section", None),
        P("section", None, "tp"),
        P("section", None, "tp"),
        P("section", "tp", None),
    )
    return jax.shard_map(
        local,
        mesh=mesh,
        in_specs=placed,
        out_specs=(
            P("section", None, "tp"),
            P("section", None, "tp"),
            P("section", None, None, "tp"),
            P("section", None, None, "tp"),
            P("section", None, None, "tp"),
        ),
        check_vma=False,
    )
```
